512 devices in a mesh: ex: 64 (over y, z_lo, core), coord: 8 (over z_hi, x).
Axes of the slice: x: 4, y: 4, z: 16 (z_hi: 2, z_lo: 8; z = z_hi * 8 + z_lo), core: 2. Of those that a mesh axis runs over, the one named last changes fastest.
Arguments:
- cotangent: bfloat16 [2048, 64, 4096], P('ex', None, 'coord'), may hold values from -0.19921875 to 0.19921875
- low_acts: bfloat16 [2048, 64, 64], P('ex'), may hold values from -6 to 6
- sign_bits: int32 [4096, 3], P('coord'), may hold values from 0 to 1073741823
- sample_blocks: int32 [64], replicated, may hold values from 0 to 2047, as said below
- bank: bfloat16 [512, 8192], P('ex', 'coord'), may hold values from -6 to 6
- target_ids: int32 [256], replicated, may hold values from 0 to 511, as said below
Outputs:
- sketches: bfloat16 [2048, 8192], P('ex', 'coord')
- scores: float32 [2048, 256], P('ex')
The draws below stay inside these ranges and needn't reach their ends.
Inputs may be any that keep to these rules, and one draw needn't show every extreme that they name: `sample_blocks`: distinct block numbers. `target_ids`: every aligned block of 8 bank rows is named by at least one id; ids may repeat, and how many rows of a block are named varies from block to block.
All inputs are finite; a program needn't handle non-finite values.
Results may differ from the reference program's by a relative error of at most 0.0049.
Values may be sent and summed in bfloat16 or wider, within the bound.
A program may use at most 64 MiB of HBM per device.

```python
import math
import jax
import jax.numpy as jnp
import numpy as np
from jax import lax

DOUT = 4096
R = 64
K = 8192
TOK = 64
EX_DEV = 32
NT = 256
BANK_DEV = 8
WORDS = 3
EXAMPLES = 2048
BANK = 512


def draw_sample_blocks(key, part):
    key = jax.random.fold_in(key, 11)
    return jax.random.permutation(key, DOUT * R // 128)[:K // 128].astype(jnp.int32)


def draw_target_ids(key, part):
    key = jax.random.fold_in(key, 23)
    owners = BANK // BANK_DEV
    first = jnp.arange(owners, dtype=jnp.int32) * BANK_DEV + jax.random.randint(jax.random.fold_in(key, 1), (owners,), 0, BANK_DEV)
    full_owner = jax.random.randint(jax.random.fold_in(key, 2), (), 0, owners)
    whole_block = full_owner * BANK_DEV + jnp.arange(BANK_DEV, dtype=jnp.int32)
    rest_count = NT - owners - BANK_DEV
    busy_count = max(owners // 2, 1)
    relabel = jax.random.permutation(jax.random.fold_in(key, 3), owners)
    busy = relabel[:busy_count]
    picked = jax.random.randint(jax.random.fold_in(key, 4), (rest_count,), 0, busy_count)
    rest = busy[picked] * BANK_DEV + jax.random.randint(jax.random.fold_in(key, 5), (rest_count,), 0, BANK_DEV)
    joined = jnp.concatenate([first.astype(jnp.int32), whole_block.astype(jnp.int32), rest.astype(jnp.int32)])
    order = jax.random.permutation(jax.random.fold_in(key, 6), NT)
    return joined[order].astype(jnp.int32)


def touch_ends(values, key, low, top_value):
    dims = values.shape
    spot = [jax.random.randint(jax.random.fold_in(key, axis), (), 0, dims[axis]) for axis in range(len(dims))]
    values = values.at[tuple(spot)].set(low)
    longest = dims.index(max(dims))
    spot[longest] = (spot[longest] + 1) % dims[longest]
    return values.at[tuple(spot)].set(top_value)


def block_scale(rng, extent, pieces, low, high):
    factor_of, own = 1.0, jax.random.fold_in(rng, 6)
    for axis_at, parts in pieces:
        heights = jnp.exp(jax.random.uniform(jax.random.fold_in(own, axis_at), (parts,), jnp.float32, low / len(pieces), high / len(pieces)))
        factor_of = factor_of * jnp.repeat(heights, extent[axis_at] // parts).reshape([-1 if axis == axis_at else 1 for axis in range(len(extent))])
    return factor_of


def scatter_about(own_key, extent, deviation, bound, cuts=(), kind=jnp.bfloat16):
    loudness = block_scale(own_key, extent, cuts, -0.22, 0.18) if cuts else 1.0
    entries = jax.random.normal(own_key, extent, jnp.float32) * deviation * loudness
    return jnp.minimum(jnp.maximum(entries, -bound), bound).astype(kind)


def setup_inputs(seed: int = 0) -> dict:
    splits = jax.random.split(jax.random.key(seed), 7)
    return {
        "cotangent": scatter_about(splits[0], (EXAMPLES, TOK, DOUT), 0.03, 0.19921875, ((0, 64), (2, 8))),
        "low_acts": scatter_about(splits[1], (EXAMPLES, TOK, R), 1.0, 6.0, ((0, 64),)),
        "sign_bits": touch_ends(jax.random.randint(splits[2], (DOUT, WORDS), 0, 1073741824), jax.random.fold_in(splits[2], 1), 0, 1073741823).astype(jnp.int32),
        "sample_blocks": draw_sample_blocks(jax.random.fold_in(splits[6], 71), 0),
        "bank": scatter_about(splits[4], (BANK, K), 1.0, 6.0, ((0, 64), (1, 8))),
        "target_ids": draw_target_ids(jax.random.fold_in(splits[6], 71), 0),
    }


def unpack_signs(sign_bits, rank):
    ranks = np.arange(rank)
    words = sign_bits[:, ranks // 30]
    shifted = jnp.right_shift(words, jnp.asarray(ranks % 30, jnp.int32)[None, :])
    return (1 - 2 * jnp.bitwise_and(shifted, 1)).astype(jnp.float32)

def hadamard_rows(values):
    batch, count = values.shape
    half = 1
    while half < count:
        shaped = values.reshape(batch, count // (2 * half), 2, half)
        upper = shaped[:, :, 0, :]
        lower = shaped[:, :, 1, :]
        values = jnp.stack([upper + lower, upper - lower], axis=2).reshape(batch, count)
        half = half * 2
    return values

def reference(cotangent, low_acts, sign_bits, sample_blocks, bank, target_ids):
    signs = unpack_signs(sign_bits, R)
    columns = (sample_blocks[:, None] * 128 + jnp.arange(128, dtype=jnp.int32)[None, :]).reshape(K).astype(jnp.int32)
    groups = EXAMPLES // EX_DEV

    def one_group(pair):
        cot_part, low_part = pair
        grads = jnp.einsum('etd,etr->edr', cot_part.astype(jnp.float32), low_part.astype(jnp.float32))
        signed = (grads * signs[None]).astype(jnp.bfloat16)
        signed = lax.optimization_barrier(signed).astype(jnp.float32)
        mixed = hadamard_rows(signed.reshape(EX_DEV, DOUT * R))
        return (jnp.take(mixed, columns, axis=1) / math.sqrt(K)).astype(jnp.bfloat16)
    sketches = lax.map(one_group, (cotangent.reshape(groups, EX_DEV, TOK, DOUT), low_acts.reshape(groups, EX_DEV, TOK, R)))
    sketches = sketches.reshape(EXAMPLES, K)
    targets = jnp.take(bank, target_ids, axis=0)
    dots = jnp.dot(sketches, targets.T, preferred_element_type=jnp.float32)
    sketch_f = sketches.astype(jnp.float32)
    target_f = targets.astype(jnp.float32)
    own = lax.optimization_barrier(jnp.sum(sketch_f * sketch_f, axis=1))
    tnorm = lax.optimization_barrier(jnp.sum(target_f * target_f, axis=1))
    scores = math.sqrt(K) * dots * lax.rsqrt(own + 1e-06)[:, None] * lax.rsqrt(tnorm + 1e-06)[None, :]
    return (sketches, scores)
```

```python
import functools
import math

import jax
import jax.numpy as jnp
from jax import lax
from jax.experimental import pallas as pl
from jax.experimental.pallas import tpu as pltpu
from jax.sharding import PartitionSpec as P

BF = jnp.bfloat16
F32 = jnp.float32
I32 = jnp.int32
MESH = pl.DeviceIdType.MESH

NX, NZH, NY, NZL, NCORE = 4, 2, 4, 8, 2
CHUNKS = 4
EX = 32
TOK = 64
RANK = 64
ODEV = 512
NSAMP = 64
NT = 256
SHARE = 1024
PAIRS = 4
COLS = PAIRS * 2 * RANK
MSG = 48


def xor(value, k):
    bit = 1
    while bit <= k:
        if k & bit:
            value = value + bit * (1 - 2 * ((value // bit) % 2))
        bit *= 2
    return value


def iota(shape, dim):
    return lax.broadcasted_iota(I32, shape, dim)


def parity_sign(v, bits):
    shift = 8
    while shift:
        if shift < bits:
            v = v ^ (v >> shift)
        shift //= 2
    return (1 - 2 * (v & 1)).astype(F32)


def dot(a, b, ca, cb):
    return lax.dot_general(a, b, (((ca,), (cb,)), ((), ())), preferred_element_type=F32)


def split(v):
    hi = v.astype(BF)
    return hi, (v - hi.astype(F32)).astype(BF)


def kernel(
    cot_hbm, low_hbm, sign_hbm, samp_hbm, bank_hbm, ids_hbm,
    sketch_ref, scores_ref,
    cot, low, sign, samp, bank, ids,
    st, had, part, xs, xr, own, zs, zr, ytmp, gath, targ, msg, mrx, mzs, mzr,
    in_sem, xs_sem, xr_sem, zs_sem, zr_sem, ls_sem, lr_sem, ys_sem, yr_sem,
    ms_sem, mr_sem, fs_sem, fr_sem,
):
    ex, co = lax.axis_index("ex"), lax.axis_index("coord")
    c, zl, y = ex % 2, (ex // 2) % NZL, ex // (2 * NZL)
    x, zh = co % NX, co // NX

    def dev_x(k):
        return (ex, zh * NX + xor(x, k))

    dev_zh = (ex, (1 - zh) * NX + x)

    def dev_zl(k):
        return ((y * NZL + xor(zl, k)) * 2 + c, co)

    def dev_yc(yk, ck):
        return ((xor(y, yk) * NZL + zl) * 2 + xor(c, ck), co)

    barrier = pltpu.get_barrier_semaphore()
    yc = [(yk, ck) for yk in range(NY) for ck in range(2) if yk or ck]
    partners = [dev_zh] + [dev_zl(k) for k in range(NZL - 1, 0, -1)]
    partners += [dev_x(k) for k in range(1, NX)] + [dev_yc(*p) for p in yc]
    for p in partners:
        pl.semaphore_signal(barrier, inc=1, device_id=p, device_id_type=MESH)

    loads = [
        pltpu.make_async_copy(src, dst, in_sem.at[n])
        for n, (src, dst) in enumerate(
            [(samp_hbm, samp), (sign_hbm, sign), (low_hbm, low), (bank_hbm, bank), (ids_hbm, ids), (cot_hbm, cot)]
        )
    ]
    for load in loads:
        load.start()

    loads[0].wait()
    rho = iota((128, 1), 0)
    share = (zh ^ ((rho // 16) % 2)) * NX + (x ^ (rho // 32))
    block = share * 8 + (rho % 16) // 2
    picked = jnp.where(iota((128, NSAMP), 1) == block, samp[...].astype(F32), 0.0)
    row = jnp.sum(picked, axis=1, keepdims=True).astype(I32) * 2 + rho % 2
    had[...] = parity_sign(row & (co * ODEV + iota((128, ODEV), 1)), 12).astype(BF)

    loads[1].wait()
    r = iota((RANK, 1), 0)
    word = jnp.where(r < 30, sign[0:1, :], jnp.where(r < 60, sign[1:2, :], sign[2:3, :]))
    shift = jnp.where(r < 30, r, jnp.where(r < 60, r - 30, r - 60))
    signs = (1 - 2 * ((word >> shift) & 1)).astype(F32)

    loads[2].wait()
    loads[3].wait()
    gath[0, 0] = jnp.concatenate([bank[:, :512], bank[:, 512:]], axis=0)
    loads[4].wait()
    loads[5].wait()

    def compute(n, _):
        for q in range(PAIRS):
            for e2 in range(2):
                e = e2 * 16 + n * PAIRS + q
                grad = dot(low[e], cot[e], 0, 0)
                at = (q * 2 + e2) * RANK
                st[at : at + RANK, :] = (grad * signs).astype(BF)
        res = dot(had[...], st[...], 1, 1)
        part[n] = res[:32]
        for k in range(1, NX):
            xs[n, k - 1] = res[32 * k : 32 * k + 32].astype(BF)
        return 0

    lax.fori_loop(0, CHUNKS, compute, 0)

    pl.semaphore_wait(barrier, len(partners))

    def remote(src, dst, ssem, rsem, to):
        return pltpu.make_async_remote_copy(
            src_ref=src, dst_ref=dst, send_sem=ssem, recv_sem=rsem, device_id=to, device_id_type=MESH
        )

    def x_copy(n, k):
        return remote(xs.at[n, k - 1], xr.at[n, k - 1], xs_sem.at[n, k - 1], xr_sem.at[n, k - 1], dev_x(k))

    def z_copy(n):
        return remote(zs.at[n], zr.at[n], zs_sem.at[n], zr_sem.at[n], dev_zh)

    def zl_copy(k):
        return remote(gath.at[0, 0], gath.at[0, k], ls_sem.at[k - 1], lr_sem.at[k - 1], dev_zl(k))

    def yc_copy(g, j):
        yk, ck = yc[j]
        four = pl.ds(g * 4, 4)
        return remote(gath.at[0, four], gath.at[j + 1, four], ys_sem.at[g, j], yr_sem.at[g, j], dev_yc(yk, ck))

    for k in (2, 1, 3):
        x_copy(0, k).start()
    for k in range(NZL - 1, 0, -1):
        zl_copy(k).start()
    for n in range(1, CHUNKS):
        for k in (2, 1, 3):
            x_copy(n, k).start()

    def x_done(n):
        for k in range(1, NX):
            x_copy(n, k).wait_recv()
        total = part[n] + xr[n, 0].astype(F32) + (xr[n, 1].astype(F32) + xr[n, 2].astype(F32))
        own[n] = total[:16]
        zs[n] = total[16:].astype(BF)
        z_copy(n).start()

    def forward(g, first):
        for k in range(first, g * 4 + 4):
            zl_copy(k).wait_recv()
        for j in range(len(yc) - 1, -1, -1):
            yc_copy(g, j).start()

    x_done(0)
    x_done(1)
    forward(0, 1)
    x_done(2)
    x_done(3)
    forward(1, 4)

    def pick(g):
        for j in range(len(yc)):
            yc_copy(g, j).wait_recv()
        rows = 8 * 64
        lane = iota((rows, 1), 0)
        i, half, slot = lane % 8, (lane // 8) % 2, lane // 16
        zk, ck, yk = slot % 4 + 4 * g, (slot // 4) % 2, slot // 8
        source = ((y ^ yk) * NZL + (zl ^ zk)) * 2 + (c ^ ck)
        match = (source * 8 + i) == ids[...]
        held = gath[:, g * 4 : g * 4 + 4].reshape(rows, 512)
        for h in range(2):
            onehot = jnp.where(match & (half == h), 1.0, 0.0).astype(BF)
            got = dot(onehot, held, 0, 0)
            if g == 0:
                targ[h] = got.astype(BF)
            else:
                targ[h] = (targ[h].astype(F32) + got).astype(BF)

    pick(0)

    a, b = iota((128, 128), 0), iota((128, 128), 1)
    small = jnp.where((a // 64) == (b // 64), parity_sign(a & b & 63, 6), 0.0).astype(BF)
    for n in range(CHUNKS):
        z_copy(n).wait_recv()
        total = own[n] + zr[n].astype(F32)
        lanes = jnp.concatenate([total[:, q * 128 : q * 128 + 128] for q in range(PAIRS)], axis=0)
        hi, lo = split(lanes)
        ytmp[n * 64 : n * 64 + 64, :] = (dot(hi, small, 1, 0) + dot(lo, small, 1, 0)) * (1.0 / math.sqrt(8192.0))
    left = iota((16, 128), 1) < 64
    for mp in range(8):
        even = ytmp[pl.ds(2 * mp, 16, stride=16), :]
        odd = ytmp[pl.ds(2 * mp + 1, 16, stride=16), :]
        top = jnp.where(left, even, pltpu.roll(odd, 64, 1))
        low_half = jnp.where(left, pltpu.roll(even, 64, 1), odd)
        sketch_ref[0:16, mp * 128 : mp * 128 + 128] = top.astype(BF)
        sketch_ref[16:32, mp * 128 : mp * 128 + 128] = low_half.astype(BF)

    ones = jnp.ones((8, 512), BF)

    def norms(values):
        v = values.astype(F32)
        hi, lo = split(v * v)
        return dot(ones, hi, 1, 1) + dot(ones, lo, 1, 1)

    sk = sketch_ref[...]
    own_norm = norms(sk[:, :512]) + norms(sk[:, 512:])

    pick(1)
    t_norm = norms(targ[0]) + norms(targ[1])
    dots = dot(sk[:, :512], targ[0], 1, 1) + dot(sk[:, 512:], targ[1], 1, 1)
    own_pad = jnp.concatenate([own_norm, jnp.zeros((8, NT - EX), F32)], axis=1)

    def pack(d, tn, on):
        thi, tlo = split(tn)
        ohi, olo = split(on)
        rr = iota((16, NT), 0)
        pick_row = lambda v: jnp.concatenate([v.astype(F32)] * 2, axis=0)
        tail = jnp.where(
            rr == 0, pick_row(thi), jnp.where(rr == 1, pick_row(tlo), jnp.where(rr == 2, pick_row(ohi), pick_row(olo)))
        )
        return jnp.concatenate([d, tail], axis=0).astype(BF)

    def m_copy(k):
        return remote(msg, mrx.at[k - 1], ms_sem.at[k - 1], mr_sem.at[k - 1], dev_x(k))

    msg[...] = pack(dots, t_norm, own_pad)
    for k in (2, 1, 3):
        m_copy(k).start()
    for k in range(1, NX):
        m_copy(k).wait_recv()
    total = (msg[...].astype(F32) + mrx[0].astype(F32)) + (mrx[1].astype(F32) + mrx[2].astype(F32))

    def unpack(m):
        return m[:EX], m[EX : EX + 1] + m[EX + 1 : EX + 2], m[EX + 2 : EX + 3] + m[EX + 3 : EX + 4]

    d, tn, on = unpack(total)
    mzs[...] = pack(d, jnp.broadcast_to(tn, (8, NT)), jnp.broadcast_to(on, (8, NT)))
    last = remote(mzs, mzr, fs_sem.at[0], fr_sem.at[0], dev_zh)
    last.start()
    last.wait_recv()
    d, tn, on = unpack(mzs[...].astype(F32) + mzr[...].astype(F32))
    diag = jnp.where(iota((EX, EX), 0) == iota((EX, EX), 1), on[:, :EX], 0.0)
    on_col = jnp.sum(diag, axis=1, keepdims=True)
    scores_ref[...] = math.sqrt(8192.0) * d * lax.rsqrt(on_col + 1e-6) * lax.rsqrt(tn + 1e-6)

    for n in range(CHUNKS):
        for k in range(1, NX):
            x_copy(n, k).wait_send()
        z_copy(n).wait_send()
    for k in range(1, NZL):
        zl_copy(k).wait_send()
    for g in range(2):
        for j in range(len(yc)):
            yc_copy(g, j).wait_send()
    for k in range(1, NX):
        m_copy(k).wait_send()
    last.wait_send()


def body(cotangent, low_acts, sign_bits, sample_blocks, bank, target_ids):
    any_spec = pl.BlockSpec(memory_space=pl.ANY)
    vmem = pl.BlockSpec(memory_space=pltpu.VMEM)
    dma = pltpu.SemaphoreType.DMA
    return pl.pallas_call(
        kernel,
        out_shape=(
            jax.ShapeDtypeStruct((EX, SHARE), BF),
            jax.ShapeDtypeStruct((EX, NT), F32),
        ),
        in_specs=[any_spec] * 6,
        out_specs=(vmem, vmem),
        scratch_shapes=[
            pltpu.VMEM((EX, TOK, ODEV), BF),
            pltpu.VMEM((EX, TOK, RANK), BF),
            pltpu.VMEM((3, ODEV), I32),
            pltpu.VMEM((1, NSAMP), I32),
            pltpu.VMEM((8, SHARE), BF),
            pltpu.VMEM((1, NT), I32),
            pltpu.VMEM((COLS, ODEV), BF),
            pltpu.VMEM((128, ODEV), BF),
            pltpu.VMEM((CHUNKS, 32, COLS), F32),
            pltpu.VMEM((CHUNKS, 3, 32, COLS), BF),
            pltpu.VMEM((CHUNKS, 3, 32, COLS), BF),
            pltpu.VMEM((CHUNKS, 16, COLS), F32),
            pltpu.VMEM((CHUNKS, 16, COLS), BF),
            pltpu.VMEM((CHUNKS, 16, COLS), BF),
            pltpu.VMEM((256, 128), F32),
            pltpu.VMEM((8, NZL, 16, 512), BF),
            pltpu.VMEM((2, NT, 512), BF),
            pltpu.VMEM((MSG, NT), BF),
            pltpu.VMEM((3, MSG, NT), BF),
            pltpu.VMEM((MSG, NT), BF),
            pltpu.VMEM((MSG, NT), BF),
            dma((6,)),
            dma((CHUNKS, 3)),
            dma((CHUNKS, 3)),
            dma((CHUNKS,)),
            dma((CHUNKS,)),
            dma((7,)),
            dma((7,)),
            dma((2, 7)),
            dma((2, 7)),
            dma((3,)),
            dma((3,)),
            dma((1,)),
            dma((1,)),
        ],
        compiler_params=pltpu.CompilerParams(
            collective_id=0, has_side_effects=True, vmem_limit_bytes=50 * 1024 * 1024
        ),
        name="sketch_scores",
    )(cotangent, low_acts, sign_bits.T, sample_blocks[None, :], bank, target_ids[None, :])


def solution(mesh):
    in_specs = (
        P("ex", None, "coord"),
        P("ex", None, None),
        P("coord", None),
        P(),
        P("ex", "coord"),
        P(),
    )
    out_specs = (P("ex", "coord"), P("ex", None))
    return jax.shard_map(body, mesh=mesh, in_specs=in_specs, out_specs=out_specs, check_vma=False)
```

```python
import functools
import math

import jax
import jax.numpy as jnp
from jax import lax
from jax.experimental import pallas as pl
from jax.experimental.pallas import tpu as pltpu
from jax.sharding import PartitionSpec as P

BF = jnp.bfloat16
F32 = jnp.float32
I32 = jnp.int32
MESH = pl.DeviceIdType.MESH

NX, NZH, NY, NZL, NCORE = 4, 2, 4, 8, 2
CHUNKS = 4
EX = 32
TOK = 64
RANK = 64
ODEV = 512
NSAMP = 64
NT = 256
SHARE = 1024
PAIRS = 4
COLS = PAIRS * 2 * RANK
MSG = 48


def xor(value, k):
    bit = 1
    while bit <= k:
        if k & bit:
            value = value + bit * (1 - 2 * ((value // bit) % 2))
        bit *= 2
    return value


def iota(shape, dim):
    return lax.broadcasted_iota(I32, shape, dim)


def parity_sign(v, bits):
    shift = 8
    while shift:
        if shift < bits:
            v = v ^ (v >> shift)
        shift //= 2
    return (1 - 2 * (v & 1)).astype(F32)


def dot(a, b, ca, cb):
    return lax.dot_general(a, b, (((ca,), (cb,)), ((), ())), preferred_element_type=F32)


def split(v):
    hi = v.astype(BF)
    return hi, (v - hi.astype(F32)).astype(BF)


def kernel(
    cot_hbm, low_hbm, sign_hbm, samp_hbm, bank_hbm, ids_hbm,
    sketch_ref, scores_ref,
    cot, low, sign, samp, bank, ids,
    st, had, part, xs, xr, own, zs, zr, ytmp, gath, targ, msg, mrx, mzs, mzr,
    in_sem, xs_sem, xr_sem, zs_sem, zr_sem, ls_sem, lr_sem, ys_sem, yr_sem,
    ms_sem, mr_sem, fs_sem, fr_sem, ready,
):
    ex, co = lax.axis_index("ex"), lax.axis_index("coord")
    c, zl, y = ex % 2, (ex // 2) % NZL, ex // (2 * NZL)
    x, zh = co % NX, co // NX

    def dev_x(k):
        return (ex, zh * NX + xor(x, k))

    dev_zh = (ex, (1 - zh) * NX + x)

    def dev_zl(k):
        return ((y * NZL + xor(zl, k)) * 2 + c, co)

    def dev_yc(yk, ck):
        return ((xor(y, yk) * NZL + zl) * 2 + xor(c, ck), co)

    barrier = pltpu.get_barrier_semaphore()
    yc = [(yk, ck) for yk in range(NY) for ck in range(2) if yk or ck]
    here = ex - c
    sibling = (here + 1 - c, co)
    far = [(here + 1, (1 - zh) * NX + x)]
    near = [((y * NZL + xor(zl, k)) * 2, co) for k in (4, 3, 2, 1)]
    near += [((xor(y, k) * NZL + zl) * 2, co) for k in range(1, NY)]
    near += [(here, zh * NX + xor(x, k)) for k in range(1, NX)]
    for p in far + near:
        pl.semaphore_signal(barrier, inc=1, device_id=p, device_id_type=MESH)

    @pl.when(c == 1)
    def _():
        pl.semaphore_signal(barrier, inc=1, device_id=sibling, device_id_type=MESH)

    loads = [
        pltpu.make_async_copy(src, dst, in_sem.at[n])
        for n, (src, dst) in enumerate(
            [(samp_hbm, samp), (sign_hbm, sign), (low_hbm, low), (bank_hbm, bank), (ids_hbm, ids), (cot_hbm, cot)]
        )
    ]
    for load in loads:
        load.start()

    loads[0].wait()
    rho = iota((128, 1), 0)
    share = (zh ^ ((rho // 16) % 2)) * NX + (x ^ (rho // 32))
    block = share * 8 + (rho % 16) // 2
    picked = jnp.where(iota((128, NSAMP), 1) == block, samp[...].astype(F32), 0.0)
    row = jnp.sum(picked, axis=1, keepdims=True).astype(I32) * 2 + rho % 2
    had[...] = parity_sign(row & (co * ODEV + iota((128, ODEV), 1)), 12).astype(BF)

    loads[1].wait()
    r = iota((RANK, 1), 0)
    word = jnp.where(r < 30, sign[0:1, :], jnp.where(r < 60, sign[1:2, :], sign[2:3, :]))
    shift = jnp.where(r < 30, r, jnp.where(r < 60, r - 30, r - 60))
    signs = (1 - 2 * ((word >> shift) & 1)).astype(F32)

    loads[2].wait()
    loads[3].wait()
    gath[0, 0] = jnp.concatenate([bank[:, :512], bank[:, 512:]], axis=0)
    loads[4].wait()
    loads[5].wait()

    def compute(n, _):
        for q in range(PAIRS):
            for e2 in range(2):
                e = e2 * 16 + n * PAIRS + q
                grad = dot(low[e], cot[e], 0, 0)
                at = (q * 2 + e2) * RANK
                st[at : at + RANK, :] = (grad * signs).astype(BF)
        res = dot(had[...], st[...], 1, 1)
        part[n] = res[:32]
        for k in range(1, NX):
            xs[n, k - 1] = res[32 * k : 32 * k + 32].astype(BF)
        return 0

    lax.fori_loop(0, CHUNKS, compute, 0)

    @pl.when(c == 0)
    def _():
        pl.semaphore_wait(barrier, 2 * len(near) + 1)
        pl.semaphore_signal(ready, inc=1, device_id=sibling, device_id_type=MESH)

    @pl.when(c == 1)
    def _():
        pl.semaphore_wait(ready, 1)

    def remote(src, dst, ssem, rsem, to):
        return pltpu.make_async_remote_copy(
            src_ref=src, dst_ref=dst, send_sem=ssem, recv_sem=rsem, device_id=to, device_id_type=MESH
        )

    def x_copy(n, k):
        return remote(xs.at[n, k - 1], xr.at[n, k - 1], xs_sem.at[n, k - 1], xr_sem.at[n, k - 1], dev_x(k))

    def z_copy(n):
        return remote(zs.at[n], zr.at[n], zs_sem.at[n], zr_sem.at[n], dev_zh)

    def zl_copy(k):
        via = k if k <= 4 else k - 4
        return remote(gath.at[0, k - via], gath.at[0, k], ls_sem.at[k - 1], lr_sem.at[k - 1], dev_zl(via))

    def yc_copy(g, j):
        yk, ck = yc[j]
        four = pl.ds(g * 4, 4)
        to = sibling if ck else dev_yc(yk, 0)
        return remote(
            gath.at[yk * 2 if ck else 0, four], gath.at[j + 1, four], ys_sem.at[g, j], yr_sem.at[g, j], to
        )

    for k in (4, 3, 2, 1):
        zl_copy(k).start()
    for n in range(CHUNKS):
        for k in (2, 1, 3):
            x_copy(n, k).start()

    def x_done(n):
        for k in range(1, NX):
            x_copy(n, k).wait_recv()
        total = part[n] + xr[n, 0].astype(F32) + (xr[n, 1].astype(F32) + xr[n, 2].astype(F32))
        own[n] = total[:16]
        zs[n] = total[16:].astype(BF)
        z_copy(n).start()

    def along_y(g):
        for j in (3, 1, 5, 0):
            yc_copy(g, j).start()

    def across(g):
        for j in (1, 3, 5):
            yc_copy(g, j).wait_recv()
            yc_copy(g, j + 1).start()

    def pick(g):
        for j in (0, 2, 4, 6):
            yc_copy(g, j).wait_recv()
        rows = 8 * 64
        lane = iota((rows, 1), 0)
        i, half, slot = lane % 8, (lane // 8) % 2, lane // 16
        zk, ck, yk = slot % 4 + 4 * g, (slot // 4) % 2, slot // 8
        source = ((y ^ yk) * NZL + (zl ^ zk)) * 2 + (c ^ ck)
        match = (source * 8 + i) == ids[...]
        held = gath[:, g * 4 : g * 4 + 4].reshape(rows, 512)
        for h in range(2):
            onehot = jnp.where(match & (half == h), 1.0, 0.0).astype(BF)
            got = dot(onehot, held, 0, 0)
            if g == 0:
                targ[h] = got.astype(BF)
            else:
                targ[h] = (targ[h].astype(F32) + got).astype(BF)

    zl_copy(4).wait_recv()
    for k in (7, 6, 5):
        zl_copy(k).start()
    for k in (1, 2, 3):
        zl_copy(k).wait_recv()
    along_y(0)

    @pl.when(c == 1)
    def _():
        pl.semaphore_wait(barrier, 2 * len(far))
        pl.semaphore_signal(ready, inc=1, device_id=sibling, device_id_type=MESH)

    @pl.when(c == 0)
    def _():
        pl.semaphore_wait(ready, 1)

    for n in range(CHUNKS):
        x_done(n)
    for k in (5, 6, 7):
        zl_copy(k).wait_recv()
    along_y(1)
    across(0)
    pick(0)
    across(1)

    a, b = iota((128, 128), 0), iota((128, 128), 1)
    small = jnp.where((a // 64) == (b // 64), parity_sign(a & b & 63, 6), 0.0).astype(BF)
    for n in range(CHUNKS):
        z_copy(n).wait_recv()
        total = own[n] + zr[n].astype(F32)
        lanes = jnp.concatenate([total[:, q * 128 : q * 128 + 128] for q in range(PAIRS)], axis=0)
        hi, lo = split(lanes)
        ytmp[n * 64 : n * 64 + 64, :] = (dot(hi, small, 1, 0) + dot(lo, small, 1, 0)) * (1.0 / math.sqrt(8192.0))
    left = iota((16, 128), 1) < 64
    for mp in range(8):
        even = ytmp[pl.ds(2 * mp, 16, stride=16), :]
        odd = ytmp[pl.ds(2 * mp + 1, 16, stride=16), :]
        top = jnp.where(left, even, pltpu.roll(odd, 64, 1))
        low_half = jnp.where(left, pltpu.roll(even, 64, 1), odd)
        sketch_ref[0:16, mp * 128 : mp * 128 + 128] = top.astype(BF)
        sketch_ref[16:32, mp * 128 : mp * 128 + 128] = low_half.astype(BF)

    ones = jnp.ones((8, 512), BF)

    def norms(values):
        v = values.astype(F32)
        hi, lo = split(v * v)
        return dot(ones, hi, 1, 1) + dot(ones, lo, 1, 1)

    sk = sketch_ref[...]
    own_norm = norms(sk[:, :512]) + norms(sk[:, 512:])

    pick(1)
    t_norm = norms(targ[0]) + norms(targ[1])
    dots = dot(sk[:, :512], targ[0], 1, 1) + dot(sk[:, 512:], targ[1], 1, 1)
    own_pad = jnp.concatenate([own_norm, jnp.zeros((8, NT - EX), F32)], axis=1)

    def pack(d, tn, on):
        thi, tlo = split(tn)
        ohi, olo = split(on)
        rr = iota((16, NT), 0)
        pick_row = lambda v: jnp.concatenate([v.astype(F32)] * 2, axis=0)
        tail = jnp.where(
            rr == 0, pick_row(thi), jnp.where(rr == 1, pick_row(tlo), jnp.where(rr == 2, pick_row(ohi), pick_row(olo)))
        )
        return jnp.concatenate([d, tail], axis=0).astype(BF)

    def m_copy(k):
        return remote(msg, mrx.at[k - 1], ms_sem.at[k - 1], mr_sem.at[k - 1], dev_x(k))

    msg[...] = pack(dots, t_norm, own_pad)
    for k in (2, 1, 3):
        m_copy(k).start()
    for k in range(1, NX):
        m_copy(k).wait_recv()
    total = (msg[...].astype(F32) + mrx[0].astype(F32)) + (mrx[1].astype(F32) + mrx[2].astype(F32))

    def unpack(m):
        return m[:EX], m[EX : EX + 1] + m[EX + 1 : EX + 2], m[EX + 2 : EX + 3] + m[EX + 3 : EX + 4]

    d, tn, on = unpack(total)
    mzs[...] = pack(d, jnp.broadcast_to(tn, (8, NT)), jnp.broadcast_to(on, (8, NT)))
    last = remote(mzs, mzr, fs_sem.at[0], fr_sem.at[0], dev_zh)
    last.start()
    last.wait_recv()
    d, tn, on = unpack(mzs[...].astype(F32) + mzr[...].astype(F32))
    diag = jnp.where(iota((EX, EX), 0) == iota((EX, EX), 1), on[:, :EX], 0.0)
    on_col = jnp.sum(diag, axis=1, keepdims=True)
    scores_ref[...] = math.sqrt(8192.0) * d * lax.rsqrt(on_col + 1e-6) * lax.rsqrt(tn + 1e-6)

    for n in range(CHUNKS):
        for k in range(1, NX):
            x_copy(n, k).wait_send()
        z_copy(n).wait_send()
    for k in range(1, NZL):
        zl_copy(k).wait_send()
    for g in range(2):
        for j in range(len(yc)):
            yc_copy(g, j).wait_send()
    for k in range(1, NX):
        m_copy(k).wait_send()
    last.wait_send()


def body(cotangent, low_acts, sign_bits, sample_blocks, bank, target_ids):
    hbm = pl.BlockSpec(memory_space=pltpu.HBM)
    vmem = pl.BlockSpec(memory_space=pltpu.VMEM)
    dma = pltpu.SemaphoreType.DMA
    return pl.pallas_call(
        kernel,
        out_shape=(
            jax.ShapeDtypeStruct((EX, SHARE), BF),
            jax.ShapeDtypeStruct((EX, NT), F32),
        ),
        in_specs=[hbm] * 6,
        out_specs=(vmem, vmem),
        scratch_shapes=[
            pltpu.VMEM((EX, TOK, ODEV), BF),
            pltpu.VMEM((EX, TOK, RANK), BF),
            pltpu.VMEM((3, ODEV), I32),
            pltpu.VMEM((1, NSAMP), I32),
            pltpu.VMEM((8, SHARE), BF),
            pltpu.VMEM((1, NT), I32),
            pltpu.VMEM((COLS, ODEV), BF),
            pltpu.VMEM((128, ODEV), BF),
            pltpu.VMEM((CHUNKS, 32, COLS), F32),
            pltpu.VMEM((CHUNKS, 3, 32, COLS), BF),
            pltpu.VMEM((CHUNKS, 3, 32, COLS), BF),
            pltpu.VMEM((CHUNKS, 16, COLS), F32),
            pltpu.VMEM((CHUNKS, 16, COLS), BF),
            pltpu.VMEM((CHUNKS, 16, COLS), BF),
            pltpu.VMEM((256, 128), F32),
            pltpu.VMEM((8, NZL, 16, 512), BF),
            pltpu.VMEM((2, NT, 512), BF),
            pltpu.VMEM((MSG, NT), BF),
            pltpu.VMEM((3, MSG, NT), BF),
            pltpu.VMEM((MSG, NT), BF),
            pltpu.VMEM((MSG, NT), BF),
            dma((6,)),
            dma((CHUNKS, 3)),
            dma((CHUNKS, 3)),
            dma((CHUNKS,)),
            dma((CHUNKS,)),
            dma((7,)),
            dma((7,)),
            dma((2, 7)),
            dma((2, 7)),
            dma((3,)),
            dma((3,)),
            dma((1,)),
            dma((1,)),
            pltpu.SemaphoreType.REGULAR,
        ],
        compiler_params=pltpu.CompilerParams(
            collective_id=0, has_side_effects=True, vmem_limit_bytes=60 * 1024 * 1024
        ),
        name="sketch_scores",
    )(cotangent, low_acts, sign_bits.T, sample_blocks[None, :], bank, target_ids[None, :])


def solution(mesh):
    in_specs = (
        P("ex", None, "coord"),
        P("ex", None, None),
        P("coord", None),
        P(),
        P("ex", "coord"),
        P(),
    )
    out_specs = (P("ex", "coord"), P("ex", None))
    return jax.shard_map(body, mesh=mesh, in_specs=in_specs, out_specs=out_specs, check_vma=False)
```

```python
import functools
import math

import jax
import jax.numpy as jnp
from jax import lax
from jax.experimental import pallas as pl
from jax.experimental.pallas import tpu as pltpu
from jax.sharding import PartitionSpec as P

BF = jnp.bfloat16
F32 = jnp.float32
I32 = jnp.int32
MESH = pl.DeviceIdType.MESH

NX, NZH, NY, NZL, NCORE = 4, 2, 4, 8, 2
CHUNKS = 4
EX = 32
TOK = 64
RANK = 64
ODEV = 512
NSAMP = 64
NT = 256
SHARE = 1024
PAIRS = 4
COLS = PAIRS * 2 * RANK
MSG = 48


def xor(value, k):
    bit = 1
    while bit <= k:
        if k & bit:
            value = value + bit * (1 - 2 * ((value // bit) % 2))
        bit *= 2
    return value


def iota(shape, dim):
    return lax.broadcasted_iota(I32, shape, dim)


def parity_sign(v, bits):
    shift = 8
    while shift:
        if shift < bits:
            v = v ^ (v >> shift)
        shift //= 2
    return (1 - 2 * (v & 1)).astype(F32)


def dot(a, b, ca, cb):
    return lax.dot_general(a, b, (((ca,), (cb,)), ((), ())), preferred_element_type=F32)


def split(v):
    hi = v.astype(BF)
    return hi, (v - hi.astype(F32)).astype(BF)


def kernel(
    cot_hbm, low_hbm, sign_hbm, samp_hbm, bank_hbm, ids_hbm,
    sketch_ref, scores_ref,
    cot, low, sign, samp, bank, ids,
    st, had, part, xs, xr, own, zs, zr, ytmp, gath, targ, msg, mrx, mzs, mzr,
    in_sem, xs_sem, xr_sem, zs_sem, zr_sem, ls_sem, lr_sem, ys_sem, yr_sem,
    ms_sem, mr_sem, fs_sem, fr_sem,
):
    ex, co = lax.axis_index("ex"), lax.axis_index("coord")
    c, zl, y = ex % 2, (ex // 2) % NZL, ex // (2 * NZL)
    x, zh = co % NX, co // NX

    def dev_x(k):
        return (ex, zh * NX + xor(x, k))

    dev_zh = (ex, (1 - zh) * NX + x)

    def dev_zl(k):
        return ((y * NZL + xor(zl, k)) * 2 + c, co)

    def dev_yc(yk, ck):
        return ((xor(y, yk) * NZL + zl) * 2 + xor(c, ck), co)

    barrier = pltpu.get_barrier_semaphore()
    yc = [(yk, ck) for yk in range(NY) for ck in range(2) if yk or ck]
    sibling = (ex + 1 - 2 * c, co)
    partners = [dev_zh] + [dev_zl(k) for k in (4, 3, 2, 1)]
    partners += [dev_yc(k, 0) for k in (2, 1, 3)] + [dev_x(k) for k in (2, 1, 3)] + [sibling]
    for p in partners:
        pl.semaphore_signal(barrier, inc=1, device_id=p, device_id_type=MESH)

    loads = [
        pltpu.make_async_copy(src, dst, in_sem.at[n])
        for n, (src, dst) in enumerate(
            [(samp_hbm, samp), (sign_hbm, sign), (low_hbm, low), (bank_hbm, bank), (ids_hbm, ids), (cot_hbm, cot)]
        )
    ]
    for load in loads:
        load.start()

    loads[0].wait()
    rho = iota((128, 1), 0)
    share = (zh ^ ((rho // 16) % 2)) * NX + (x ^ (rho // 32))
    block = share * 8 + (rho % 16) // 2
    picked = jnp.where(iota((128, NSAMP), 1) == block, samp[...].astype(F32), 0.0)
    row = jnp.sum(picked, axis=1, keepdims=True).astype(I32) * 2 + rho % 2
    had[...] = parity_sign(row & (co * ODEV + iota((128, ODEV), 1)), 12).astype(BF)

    loads[1].wait()
    r = iota((RANK, 1), 0)
    word = jnp.where(r < 30, sign[0:1, :], jnp.where(r < 60, sign[1:2, :], sign[2:3, :]))
    shift = jnp.where(r < 30, r, jnp.where(r < 60, r - 30, r - 60))
    signs = (1 - 2 * ((word >> shift) & 1)).astype(F32)

    loads[2].wait()
    loads[3].wait()
    gath[0, 0] = jnp.concatenate([bank[:, :512], bank[:, 512:]], axis=0)
    loads[4].wait()
    loads[5].wait()

    def compute(n, _):
        for q in range(PAIRS):
            for e2 in range(2):
                e = e2 * 16 + n * PAIRS + q
                grad = dot(low[e], cot[e], 0, 0)
                at = (q * 2 + e2) * RANK
                st[at : at + RANK, :] = (grad * signs).astype(BF)
        res = dot(had[...], st[...], 1, 1)
        part[n] = res[:32]
        for k in range(1, NX):
            xs[n, k - 1] = res[32 * k : 32 * k + 32].astype(BF)
        return 0

    lax.fori_loop(0, CHUNKS, compute, 0)
    pl.semaphore_wait(barrier, len(partners))

    def remote(src, dst, ssem, rsem, to):
        return pltpu.make_async_remote_copy(
            src_ref=src, dst_ref=dst, send_sem=ssem, recv_sem=rsem, device_id=to, device_id_type=MESH
        )

    def x_copy(n, k):
        return remote(xs.at[n, k - 1], xr.at[n, k - 1], xs_sem.at[n, k - 1], xr_sem.at[n, k - 1], dev_x(k))

    def z_copy(n):
        return remote(zs.at[n], zr.at[n], zs_sem.at[n], zr_sem.at[n], dev_zh)

    def zl_copy(k):
        via = k if k <= 4 else k - 4
        return remote(gath.at[0, k - via], gath.at[0, k], ls_sem.at[k - 1], lr_sem.at[k - 1], dev_zl(via))

    def yc_copy(g, j):
        yk, ck = yc[j]
        four = pl.ds(g * 4, 4)
        to = sibling if ck else dev_yc(yk, 0)
        return remote(
            gath.at[yk * 2 if ck else 0, four], gath.at[j + 1, four], ys_sem.at[g, j], yr_sem.at[g, j], to
        )

    for k in (4, 3, 2, 1):
        zl_copy(k).start()
    def x_start(n):
        for k in (2, 1, 3):
            x_copy(n, k).start()

    for n in range(CHUNKS):
        x_start(n)

    def x_done(n):
        for k in range(1, NX):
            x_copy(n, k).wait_recv()
        total = part[n] + xr[n, 0].astype(F32) + (xr[n, 1].astype(F32) + xr[n, 2].astype(F32))
        own[n] = total[:16]
        zs[n] = total[16:].astype(BF)
        z_copy(n).start()

    def along_y(g):
        for j in (3, 1, 5, 0):
            yc_copy(g, j).start()

    def across(g):
        for j in (1, 3, 5):
            yc_copy(g, j).wait_recv()
            yc_copy(g, j + 1).start()

    def pick(g):
        for j in (0, 2, 4, 6):
            yc_copy(g, j).wait_recv()
        rows = 8 * 64
        lane = iota((rows, 1), 0)
        i, half, slot = lane % 8, (lane // 8) % 2, lane // 16
        zk, ck, yk = slot % 4 + 4 * g, (slot // 4) % 2, slot // 8
        source = ((y ^ yk) * NZL + (zl ^ zk)) * 2 + (c ^ ck)
        match = (source * 8 + i) == ids[...]
        held = gath[:, g * 4 : g * 4 + 4].reshape(rows, 512)
        for h in range(2):
            onehot = jnp.where(match & (half == h), 1.0, 0.0).astype(BF)
            got = dot(onehot, held, 0, 0)
            if g == 0:
                targ[h] = got.astype(BF)
            else:
                targ[h] = (targ[h].astype(F32) + got).astype(BF)

    x_done(0)
    zl_copy(4).wait_recv()
    for k in (7, 6, 5):
        zl_copy(k).start()
    for k in (1, 2, 3):
        zl_copy(k).wait_recv()
    along_y(0)
    for n in range(1, CHUNKS):
        x_done(n)
    for k in (5, 6, 7):
        zl_copy(k).wait_recv()
    along_y(1)
    across(0)
    pick(0)
    across(1)

    a, b = iota((128, 128), 0), iota((128, 128), 1)
    small = jnp.where((a // 64) == (b // 64), parity_sign(a & b & 63, 6), 0.0).astype(BF)
    for n in range(CHUNKS):
        z_copy(n).wait_recv()
        total = own[n] + zr[n].astype(F32)
        lanes = jnp.concatenate([total[:, q * 128 : q * 128 + 128] for q in range(PAIRS)], axis=0)
        hi, lo = split(lanes)
        ytmp[n * 64 : n * 64 + 64, :] = (dot(hi, small, 1, 0) + dot(lo, small, 1, 0)) * (1.0 / math.sqrt(8192.0))
    left = iota((16, 128), 1) < 64
    for mp in range(8):
        even = ytmp[pl.ds(2 * mp, 16, stride=16), :]
        odd = ytmp[pl.ds(2 * mp + 1, 16, stride=16), :]
        top = jnp.where(left, even, pltpu.roll(odd, 64, 1))
        low_half = jnp.where(left, pltpu.roll(even, 64, 1), odd)
        sketch_ref[0:16, mp * 128 : mp * 128 + 128] = top.astype(BF)
        sketch_ref[16:32, mp * 128 : mp * 128 + 128] = low_half.astype(BF)

    ones = jnp.ones((8, 512), BF)

    def norms(values):
        v = values.astype(F32)
        hi, lo = split(v * v)
        return dot(ones, hi, 1, 1) + dot(ones, lo, 1, 1)

    sk = sketch_ref[...]
    own_norm = norms(sk[:, :512]) + norms(sk[:, 512:])

    pick(1)
    t_norm = norms(targ[0]) + norms(targ[1])
    dots = dot(sk[:, :512], targ[0], 1, 1) + dot(sk[:, 512:], targ[1], 1, 1)
    own_pad = jnp.concatenate([own_norm, jnp.zeros((8, NT - EX), F32)], axis=1)

    def pack(d, tn, on):
        thi, tlo = split(tn)
        ohi, olo = split(on)
        rr = iota((16, NT), 0)
        pick_row = lambda v: jnp.concatenate([v.astype(F32)] * 2, axis=0)
        tail = jnp.where(
            rr == 0, pick_row(thi), jnp.where(rr == 1, pick_row(tlo), jnp.where(rr == 2, pick_row(ohi), pick_row(olo)))
        )
        return jnp.concatenate([d, tail], axis=0).astype(BF)

    def m_copy(k):
        return remote(msg, mrx.at[k - 1], ms_sem.at[k - 1], mr_sem.at[k - 1], dev_x(k))

    msg[...] = pack(dots, t_norm, own_pad)
    for k in (2, 1, 3):
        m_copy(k).start()
    for k in range(1, NX):
        m_copy(k).wait_recv()
    total = (msg[...].astype(F32) + mrx[0].astype(F32)) + (mrx[1].astype(F32) + mrx[2].astype(F32))

    def unpack(m):
        return m[:EX], m[EX : EX + 1] + m[EX + 1 : EX + 2], m[EX + 2 : EX + 3] + m[EX + 3 : EX + 4]

    d, tn, on = unpack(total)
    mzs[...] = pack(d, jnp.broadcast_to(tn, (8, NT)), jnp.broadcast_to(on, (8, NT)))
    last = remote(mzs, mzr, fs_sem.at[0], fr_sem.at[0], dev_zh)
    last.start()
    last.wait_recv()
    d, tn, on = unpack(mzs[...].astype(F32) + mzr[...].astype(F32))
    diag = jnp.where(iota((EX, EX), 0) == iota((EX, EX), 1), on[:, :EX], 0.0)
    on_col = jnp.sum(diag, axis=1, keepdims=True)
    scores_ref[...] = math.sqrt(8192.0) * d * lax.rsqrt(on_col + 1e-6) * lax.rsqrt(tn + 1e-6)

    for n in range(CHUNKS):
        for k in range(1, NX):
            x_copy(n, k).wait_send()
        z_copy(n).wait_send()
    for k in range(1, NZL):
        zl_copy(k).wait_send()
    for g in range(2):
        for j in range(len(yc)):
            yc_copy(g, j).wait_send()
    for k in range(1, NX):
        m_copy(k).wait_send()
    last.wait_send()


def body(cotangent, low_acts, sign_bits, sample_blocks, bank, target_ids):
    hbm = pl.BlockSpec(memory_space=pltpu.HBM)
    vmem = pl.BlockSpec(memory_space=pltpu.VMEM)
    dma = pltpu.SemaphoreType.DMA
    return pl.pallas_call(
        kernel,
        out_shape=(
            jax.ShapeDtypeStruct((EX, SHARE), BF),
            jax.ShapeDtypeStruct((EX, NT), F32),
        ),
        in_specs=[hbm] * 6,
        out_specs=(vmem, vmem),
        scratch_shapes=[
            pltpu.VMEM((EX, TOK, ODEV), BF),
            pltpu.VMEM((EX, TOK, RANK), BF),
            pltpu.VMEM((3, ODEV), I32),
            pltpu.VMEM((1, NSAMP), I32),
            pltpu.VMEM((8, SHARE), BF),
            pltpu.VMEM((1, NT), I32),
            pltpu.VMEM((COLS, ODEV), BF),
            pltpu.VMEM((128, ODEV), BF),
            pltpu.VMEM((CHUNKS, 32, COLS), F32),
            pltpu.VMEM((CHUNKS, 3, 32, COLS), BF),
            pltpu.VMEM((CHUNKS, 3, 32, COLS), BF),
            pltpu.VMEM((CHUNKS, 16, COLS), F32),
            pltpu.VMEM((CHUNKS, 16, COLS), BF),
            pltpu.VMEM((CHUNKS, 16, COLS), BF),
            pltpu.VMEM((256, 128), F32),
            pltpu.VMEM((8, NZL, 16, 512), BF),
            pltpu.VMEM((2, NT, 512), BF),
            pltpu.VMEM((MSG, NT), BF),
            pltpu.VMEM((3, MSG, NT), BF),
            pltpu.VMEM((MSG, NT), BF),
            pltpu.VMEM((MSG, NT), BF),
            dma((6,)),
            dma((CHUNKS, 3)),
            dma((CHUNKS, 3)),
            dma((CHUNKS,)),
            dma((CHUNKS,)),
            dma((7,)),
            dma((7,)),
            dma((2, 7)),
            dma((2, 7)),
            dma((3,)),
            dma((3,)),
            dma((1,)),
            dma((1,)),
        ],
        compiler_params=pltpu.CompilerParams(
            collective_id=0, has_side_effects=True, vmem_limit_bytes=60 * 1024 * 1024
        ),
        name="sketch_scores",
    )(cotangent, low_acts, sign_bits.T, sample_blocks[None, :], bank, target_ids[None, :])


def solution(mesh):
    in_specs = (
        P("ex", None, "coord"),
        P("ex", None, None),
        P("coord", None),
        P(),
        P("ex", "coord"),
        P(),
    )
    out_specs = (P("ex", "coord"), P("ex", None))
    return jax.shard_map(body, mesh=mesh, in_specs=in_specs, out_specs=out_specs, check_vma=False)
```

```python
import functools
import math

import jax
import jax.numpy as jnp
from jax import lax
from jax.experimental import pallas as pl
from jax.experimental.pallas import tpu as pltpu
from jax.sharding import PartitionSpec as P

BF = jnp.bfloat16
F32 = jnp.float32
I32 = jnp.int32
MESH = pl.DeviceIdType.MESH

NX, NZH, NY, NZL, NCORE = 4, 2, 4, 8, 2
CHUNKS = 4
EX = 32
TOK = 64
RANK = 64
ODEV = 512
NSAMP = 64
NT = 256
SHARE = 1024
PAIRS = 4
COLS = PAIRS * 2 * RANK
MSG = 48


def xor(value, k):
    bit = 1
    while bit <= k:
        if k & bit:
            value = value + bit * (1 - 2 * ((value // bit) % 2))
        bit *= 2
    return value


def iota(shape, dim):
    return lax.broadcasted_iota(I32, shape, dim)


def parity_sign(v, bits):
    shift = 8
    while shift:
        if shift < bits:
            v = v ^ (v >> shift)
        shift //= 2
    return (1 - 2 * (v & 1)).astype(F32)


def dot(a, b, ca, cb):
    return lax.dot_general(a, b, (((ca,), (cb,)), ((), ())), preferred_element_type=F32)


def split(v):
    hi = v.astype(BF)
    return hi, (v - hi.astype(F32)).astype(BF)


def kernel(
    cot_hbm, low_hbm, sign_hbm, samp_hbm, bank_hbm, ids_hbm,
    sketch_ref, scores_ref,
    cot, low, sign, samp, bank, ids,
    st, had, part, xs, xr, own, zs, zr, ytmp, gath, targ, msg, mrx, mzs, mzr,
    in_sem, xs_sem, xr_sem, zs_sem, zr_sem, ls_sem, lr_sem, ys_sem, yr_sem,
    ms_sem, mr_sem, fs_sem, fr_sem,
):
    ex, co = lax.axis_index("ex"), lax.axis_index("coord")
    c, zl, y = ex % 2, (ex // 2) % NZL, ex // (2 * NZL)
    x, zh = co % NX, co // NX

    def dev_x(k):
        return (ex, zh * NX + xor(x, k))

    dev_zh = (ex, (1 - zh) * NX + x)

    def dev_zl(k):
        return ((y * NZL + xor(zl, k)) * 2 + c, co)

    def dev_yc(yk, ck):
        return ((xor(y, yk) * NZL + zl) * 2 + xor(c, ck), co)

    barrier = pltpu.get_barrier_semaphore()
    yc = [(yk, ck) for yk in range(NY) for ck in range(2) if yk or ck]
    sibling = (ex + 1 - 2 * c, co)
    partners = [dev_zh] + [dev_zl(k) for k in (4, 3, 2, 1)]
    partners += [dev_yc(k, 0) for k in (2, 1, 3)] + [dev_x(k) for k in (2, 1, 3)] + [sibling]
    for p in partners:
        pl.semaphore_signal(barrier, inc=1, device_id=p, device_id_type=MESH)

    loads = [
        pltpu.make_async_copy(src, dst, in_sem.at[n])
        for n, (src, dst) in enumerate(
            [(samp_hbm, samp), (sign_hbm, sign), (low_hbm, low), (bank_hbm, bank), (ids_hbm, ids), (cot_hbm, cot)]
        )
    ]
    for load in loads:
        load.start()

    loads[0].wait()
    rho = iota((128, 1), 0)
    share = (zh ^ ((rho // 16) % 2)) * NX + (x ^ (rho // 32))
    block = share * 8 + (rho % 16) // 2
    picked = jnp.where(iota((128, NSAMP), 1) == block, samp[...].astype(F32), 0.0)
    row = jnp.sum(picked, axis=1, keepdims=True).astype(I32) * 2 + rho % 2
    had[...] = parity_sign(row & (co * ODEV + iota((128, ODEV), 1)), 12).astype(BF)

    loads[1].wait()
    r = iota((RANK, 1), 0)
    word = jnp.where(r < 30, sign[0:1, :], jnp.where(r < 60, sign[1:2, :], sign[2:3, :]))
    shift = jnp.where(r < 30, r, jnp.where(r < 60, r - 30, r - 60))
    signs = (1 - 2 * ((word >> shift) & 1)).astype(F32)

    loads[2].wait()
    loads[3].wait()
    gath[0, 0] = jnp.concatenate([bank[:, :512], bank[:, 512:]], axis=0)
    loads[4].wait()
    loads[5].wait()

    def compute(n, _):
        for q in range(PAIRS):
            for e2 in range(2):
                e = e2 * 16 + n * PAIRS + q
                grad = dot(low[e], cot[e], 0, 0)
                at = (q * 2 + e2) * RANK
                st[at : at + RANK, :] = (grad * signs).astype(BF)
        res = dot(had[...], st[...], 1, 1)
        part[n] = res[:32]
        for k in range(1, NX):
            xs[n, k - 1] = res[32 * k : 32 * k + 32].astype(BF)
        return 0

    lax.fori_loop(0, CHUNKS, compute, 0)
    pl.semaphore_wait(barrier, len(partners))

    def remote(src, dst, ssem, rsem, to):
        return pltpu.make_async_remote_copy(
            src_ref=src, dst_ref=dst, send_sem=ssem, recv_sem=rsem, device_id=to, device_id_type=MESH
        )

    def x_copy(n, k):
        return remote(xs.at[n, k - 1], xr.at[n, k - 1], xs_sem.at[n, k - 1], xr_sem.at[n, k - 1], dev_x(k))

    def z_copy(n):
        return remote(zs.at[n], zr.at[n], zs_sem.at[n], zr_sem.at[n], dev_zh)

    def zl_copy(k):
        via = k if k <= 4 else k - 4
        return remote(gath.at[0, k - via], gath.at[0, k], ls_sem.at[k - 1], lr_sem.at[k - 1], dev_zl(via))

    def yc_copy(g, j):
        yk, ck = yc[j]
        four = pl.ds(g * 4, 4)
        to = sibling if ck else dev_yc(yk, 0)
        return remote(
            gath.at[yk * 2 if ck else 0, four], gath.at[j + 1, four], ys_sem.at[g, j], yr_sem.at[g, j], to
        )

    for k in (4, 3, 2, 1):
        zl_copy(k).start()
    def x_start(n):
        for k in (2, 1, 3):
            x_copy(n, k).start()

    for n in range(CHUNKS):
        x_start(n)

    def x_done(n):
        for k in range(1, NX):
            x_copy(n, k).wait_recv()
        total = part[n] + xr[n, 0].astype(F32) + (xr[n, 1].astype(F32) + xr[n, 2].astype(F32))
        own[n] = total[:16]
        zs[n] = total[16:].astype(BF)
        z_copy(n).start()

    def along_y(g):
        for j in (3, 1, 5, 0):
            yc_copy(g, j).start()

    def across(g):
        for j in (1, 3, 5):
            yc_copy(g, j).wait_recv()
            yc_copy(g, j + 1).start()

    def pick(g):
        for j in (0, 2, 4, 6):
            yc_copy(g, j).wait_recv()
        rows = 8 * 64
        lane = iota((rows, 1), 0)
        i, half, slot = lane % 8, (lane // 8) % 2, lane // 16
        zk, ck, yk = slot % 4 + 4 * g, (slot // 4) % 2, slot // 8
        source = ((y ^ yk) * NZL + (zl ^ zk)) * 2 + (c ^ ck)
        match = (source * 8 + i) == ids[...]
        held = gath[:, g * 4 : g * 4 + 4].reshape(rows, 512)
        for h in range(2):
            onehot = jnp.where(match & (half == h), 1.0, 0.0).astype(BF)
            got = dot(onehot, held, 0, 0)
            if g == 0:
                targ[h] = got.astype(BF)
            else:
                targ[h] = (targ[h].astype(F32) + got).astype(BF)

    x_done(0)
    zl_copy(4).wait_recv()
    for k in (7, 6, 5):
        zl_copy(k).start()
    x_done(1)
    for k in (1, 2, 3):
        zl_copy(k).wait_recv()
    along_y(0)
    for n in range(2, CHUNKS):
        x_done(n)
    for k in (5, 6, 7):
        zl_copy(k).wait_recv()
    along_y(1)
    across(0)
    pick(0)
    across(1)

    a, b = iota((128, 128), 0), iota((128, 128), 1)
    small = jnp.where((a // 64) == (b // 64), parity_sign(a & b & 63, 6), 0.0).astype(BF)
    for n in range(CHUNKS):
        z_copy(n).wait_recv()
        total = own[n] + zr[n].astype(F32)
        lanes = jnp.concatenate([total[:, q * 128 : q * 128 + 128] for q in range(PAIRS)], axis=0)
        hi, lo = split(lanes)
        ytmp[n * 64 : n * 64 + 64, :] = (dot(hi, small, 1, 0) + dot(lo, small, 1, 0)) * (1.0 / math.sqrt(8192.0))
    left = iota((16, 128), 1) < 64
    for mp in range(8):
        even = ytmp[pl.ds(2 * mp, 16, stride=16), :]
        odd = ytmp[pl.ds(2 * mp + 1, 16, stride=16), :]
        top = jnp.where(left, even, pltpu.roll(odd, 64, 1))
        low_half = jnp.where(left, pltpu.roll(even, 64, 1), odd)
        sketch_ref[0:16, mp * 128 : mp * 128 + 128] = top.astype(BF)
        sketch_ref[16:32, mp * 128 : mp * 128 + 128] = low_half.astype(BF)

    ones = jnp.ones((8, 512), BF)

    def norms(values):
        v = values.astype(F32)
        hi, lo = split(v * v)
        return dot(ones, hi, 1, 1) + dot(ones, lo, 1, 1)

    sk = sketch_ref[...]
    own_norm = norms(sk[:, :512]) + norms(sk[:, 512:])

    pick(1)
    t_norm = norms(targ[0]) + norms(targ[1])
    dots = dot(sk[:, :512], targ[0], 1, 1) + dot(sk[:, 512:], targ[1], 1, 1)
    own_pad = jnp.concatenate([own_norm, jnp.zeros((8, NT - EX), F32)], axis=1)

    def pack(d, tn, on):
        thi, tlo = split(tn)
        ohi, olo = split(on)
        rr = iota((16, NT), 0)
        pick_row = lambda v: jnp.concatenate([v.astype(F32)] * 2, axis=0)
        tail = jnp.where(
            rr == 0, pick_row(thi), jnp.where(rr == 1, pick_row(tlo), jnp.where(rr == 2, pick_row(ohi), pick_row(olo)))
        )
        return jnp.concatenate([d, tail], axis=0).astype(BF)

    def m_copy(k):
        return remote(msg, mrx.at[k - 1], ms_sem.at[k - 1], mr_sem.at[k - 1], dev_x(k))

    msg[...] = pack(dots, t_norm, own_pad)
    for k in (2, 1, 3):
        m_copy(k).start()
    for k in range(1, NX):
        m_copy(k).wait_recv()
    total = (msg[...].astype(F32) + mrx[0].astype(F32)) + (mrx[1].astype(F32) + mrx[2].astype(F32))

    def unpack(m):
        return m[:EX], m[EX : EX + 1] + m[EX + 1 : EX + 2], m[EX + 2 : EX + 3] + m[EX + 3 : EX + 4]

    d, tn, on = unpack(total)
    mzs[...] = pack(d, jnp.broadcast_to(tn, (8, NT)), jnp.broadcast_to(on, (8, NT)))
    last = remote(mzs, mzr, fs_sem.at[0], fr_sem.at[0], dev_zh)
    last.start()
    last.wait_recv()
    d, tn, on = unpack(mzs[...].astype(F32) + mzr[...].astype(F32))
    diag = jnp.where(iota((EX, EX), 0) == iota((EX, EX), 1), on[:, :EX], 0.0)
    on_col = jnp.sum(diag, axis=1, keepdims=True)
    scores_ref[...] = math.sqrt(8192.0) * d * lax.rsqrt(on_col + 1e-6) * lax.rsqrt(tn + 1e-6)

    for n in range(CHUNKS):
        for k in range(1, NX):
            x_copy(n, k).wait_send()
        z_copy(n).wait_send()
    for k in range(1, NZL):
        zl_copy(k).wait_send()
    for g in range(2):
        for j in range(len(yc)):
            yc_copy(g, j).wait_send()
    for k in range(1, NX):
        m_copy(k).wait_send()
    last.wait_send()


def body(cotangent, low_acts, sign_bits, sample_blocks, bank, target_ids):
    hbm = pl.BlockSpec(memory_space=pltpu.HBM)
    vmem = pl.BlockSpec(memory_space=pltpu.VMEM)
    dma = pltpu.SemaphoreType.DMA
    return pl.pallas_call(
        kernel,
        out_shape=(
            jax.ShapeDtypeStruct((EX, SHARE), BF),
            jax.ShapeDtypeStruct((EX, NT), F32),
        ),
        in_specs=[hbm] * 6,
        out_specs=(vmem, vmem),
        scratch_shapes=[
            pltpu.VMEM((EX, TOK, ODEV), BF),
            pltpu.VMEM((EX, TOK, RANK), BF),
            pltpu.VMEM((3, ODEV), I32),
            pltpu.VMEM((1, NSAMP), I32),
            pltpu.VMEM((8, SHARE), BF),
            pltpu.VMEM((1, NT), I32),
            pltpu.VMEM((COLS, ODEV), BF),
            pltpu.VMEM((128, ODEV), BF),
            pltpu.VMEM((CHUNKS, 32, COLS), F32),
            pltpu.VMEM((CHUNKS, 3, 32, COLS), BF),
            pltpu.VMEM((CHUNKS, 3, 32, COLS), BF),
            pltpu.VMEM((CHUNKS, 16, COLS), F32),
            pltpu.VMEM((CHUNKS, 16, COLS), BF),
            pltpu.VMEM((CHUNKS, 16, COLS), BF),
            pltpu.VMEM((256, 128), F32),
            pltpu.VMEM((8, NZL, 16, 512), BF),
            pltpu.VMEM((2, NT, 512), BF),
            pltpu.VMEM((MSG, NT), BF),
            pltpu.VMEM((3, MSG, NT), BF),
            pltpu.VMEM((MSG, NT), BF),
            pltpu.VMEM((MSG, NT), BF),
            dma((6,)),
            dma((CHUNKS, 3)),
            dma((CHUNKS, 3)),
            dma((CHUNKS,)),
            dma((CHUNKS,)),
            dma((7,)),
            dma((7,)),
            dma((2, 7)),
            dma((2, 7)),
            dma((3,)),
            dma((3,)),
            dma((1,)),
            dma((1,)),
        ],
        compiler_params=pltpu.CompilerParams(
            collective_id=0, has_side_effects=True, vmem_limit_bytes=60 * 1024 * 1024
        ),
        name="sketch_scores",
    )(cotangent, low_acts, sign_bits.T, sample_blocks[None, :], bank, target_ids[None, :])


def solution(mesh):
    in_specs = (
        P("ex", None, "coord"),
        P("ex", None, None),
        P("coord", None),
        P(),
        P("ex", "coord"),
        P(),
    )
    out_specs = (P("ex", "coord"), P("ex", None))
    return jax.shard_map(body, mesh=mesh, in_specs=in_specs, out_specs=out_specs, check_vma=False)
```
